32 devices in a mesh: seq: 8 (over z, core), dp: 4 (over y, x).
Axes of the slice: x: 2, y: 2, z: 4, core: 2. Of those that a mesh axis runs over, the one named last changes fastest.
Arguments:
- query: bfloat16 [4096, 8192], P(('dp', 'seq')), parts along dimension 0, may hold values from -5 to 5
- keys: bfloat16 [4096, 1024], P(('dp', 'seq')), parts along dimension 0, may hold values from -7 to 7
- values: bfloat16 [4096, 1024], P(('dp', 'seq')), parts along dimension 0, may hold values from -5 to 5
- out_grad: bfloat16 [4096, 8192], P(('dp', 'seq')), parts along dimension 0, may hold values from -5 to 5
Outputs:
- attended: bfloat16 [4096, 8192], P(('dp', 'seq')), parts along dimension 0
- query_grad: bfloat16 [4096, 8192], P(('dp', 'seq')), parts along dimension 0
- key_grad: bfloat16 [4096, 1024], P(('dp', 'seq')), parts along dimension 0
- value_grad: bfloat16 [4096, 1024], P(('dp', 'seq')), parts along dimension 0
The draws below stay inside these ranges and needn't reach their ends.
There are 4 independent parts, one for each index of `dp`. The reference program is written for one: setup_inputs(seed, part) draws one part's arguments, and reference() takes and returns one part's arrays. A program takes and returns all parts, laid end to end along the dimension named above; each array names one. Nothing has to cross between parts.
All inputs are finite; a program needn't handle non-finite values.
Results may differ from the reference program's by a relative error of at most 0.025.
Values may be sent and summed in bfloat16 or wider, within the bound.
No kernel may reach another device: no remote copies, remote signals or barrier semaphores. Data moves between devices by JAX's collectives and lax.ppermute only.
A program may use at most 192 MiB of HBM per device.

```python
import jax
import jax.numpy as jnp
from jax import lax

HQ = 64
KVH = 8
HD = 128
SEQ = 1024


def draw_query(key, part):
    key = jax.random.fold_in(key, 11)
    result = jnp.clip(jax.random.normal(key, (SEQ, HQ * HD), jnp.float32), -4.0, 4.0)
    return result.astype(jnp.bfloat16)


def draw_keys(key, part):
    key = jax.random.fold_in(key, 12)
    result = jnp.clip(jax.random.normal(key, (SEQ, KVH * HD), jnp.float32), -4.0, 4.0)
    return result.astype(jnp.bfloat16)


def shard_levels(stream_key, shape, pieces, low, high):
    loudness = 1.0
    for dim, shards_of in pieces:
        draws = jax.random.uniform(jax.random.fold_in(jax.random.fold_in(stream_key, 6), dim), (shards_of,), jnp.float32, low / len(pieces), high / len(pieces))
        loudness = loudness * jnp.repeat(jnp.exp(draws), shape[dim] // shards_of).reshape((-1,) + (1,) * (len(shape) - 1 - dim))
    return loudness


def noise(stream_key, dims, width, limit, shards=(), kind=jnp.bfloat16):
    gain = shard_levels(stream_key, dims, shards, -0.22, 0.18) if shards else 1.0
    drawn = jax.random.normal(stream_key, dims, jnp.float32) * width * gain
    return jnp.minimum(jnp.maximum(drawn, -limit), limit).astype(kind)


def setup_inputs(seed: int = 0, part: int = 0) -> dict:
    arg_keys = jax.random.split(jax.random.key(seed), 5)
    own_keys = jax.random.split(jax.random.fold_in(arg_keys[4], part), 5)
    return {
        "query": draw_query(jax.random.fold_in(jax.random.fold_in(arg_keys[4], part), 71), part),
        "keys": draw_keys(jax.random.fold_in(jax.random.fold_in(arg_keys[4], part), 71), part),
        "values": noise(own_keys[2], (SEQ, KVH * HD), 1.0, 5.0, ((0, 8),)),
        "out_grad": noise(own_keys[3], (SEQ, HQ * HD), 1.0, 5.0, ((0, 8),)),
    }


def attend_group(query_group, key_group, value_group, grad_group):
    scaling = HD ** -0.5
    query_f = query_group.astype(jnp.float32)
    key_f = key_group.astype(jnp.float32)
    value_f = value_group.astype(jnp.float32)
    grad_f = grad_group.astype(jnp.float32)
    scores = jnp.einsum('qhd,kd->hqk', query_f, key_f) * scaling
    positions = jnp.arange(SEQ)
    visible = positions[:, None] >= positions[None, :]
    scores = jnp.where(visible[None], scores, -jnp.inf)
    peak_score = jnp.max(scores, axis=-1, keepdims=True)
    expo = jnp.exp(scores - peak_score)
    weights = expo / jnp.sum(expo, axis=-1, keepdims=True)
    weights_low = weights.astype(jnp.bfloat16)
    attended = jnp.einsum('hqk,kd->qhd', weights_low.astype(jnp.float32), value_f).astype(jnp.bfloat16)
    weight_grads = jnp.einsum('qhd,kd->hqk', grad_f, value_f)
    row_dots = jnp.sum(grad_f * attended.astype(jnp.float32), axis=-1).T[:, :, None]
    score_grads = (weights * (weight_grads - row_dots) * scaling).astype(jnp.bfloat16)
    score_f = score_grads.astype(jnp.float32)
    query_grad = jnp.einsum('hqk,kd->qhd', score_f, key_f).astype(jnp.bfloat16)
    key_grad = jnp.einsum('hqk,qhd->kd', score_f, query_f).astype(jnp.bfloat16)
    value_grad = jnp.einsum('hqk,qhd->kd', weights_low.astype(jnp.float32), grad_f).astype(jnp.bfloat16)
    return attended, query_grad, key_grad, value_grad


def reference(query, keys, values, out_grad):
    group = HQ // KVH
    query_groups = query.reshape(SEQ, KVH, group, HD).transpose(1, 0, 2, 3)
    grad_groups = out_grad.reshape(SEQ, KVH, group, HD).transpose(1, 0, 2, 3)
    key_groups = keys.reshape(SEQ, KVH, HD).transpose(1, 0, 2)
    value_groups = values.reshape(SEQ, KVH, HD).transpose(1, 0, 2)
    results = lax.map(lambda packed: attend_group(*packed), (query_groups, key_groups, value_groups, grad_groups))
    attended = results[0].transpose(1, 0, 2, 3).reshape(SEQ, HQ * HD)
    query_grad = results[1].transpose(1, 0, 2, 3).reshape(SEQ, HQ * HD)
    key_grad = results[2].transpose(1, 0, 2).reshape(SEQ, KVH * HD)
    value_grad = results[3].transpose(1, 0, 2).reshape(SEQ, KVH * HD)
    return (attended, query_grad, key_grad, value_grad)
```

```python
import functools

import jax
import jax.numpy as jnp
from jax import lax
from jax.experimental import pallas as pl
from jax.experimental.pallas import tpu as pltpu
from jax.sharding import PartitionSpec as P

KVH = 8
HD = 128
CORES = 2
LOG2E = 1.4426950408889634
GROUPS = (1, 1, 1, 1)


def dot(a, b, dims=(((1,), (0,)), ((), ()))):
    return lax.dot_general(a, b, dims, preferred_element_type=jnp.float32)


NT = (((1,), (1,)), ((), ()))


def attention_kernel(chips, heads, n_alias, place, *refs):
    q_own, q_sib, g_own, g_sib = refs[:4]
    kv = refs[4 : 4 + chips]
    outs = refs[4 + chips + n_alias :]
    att_own, dq_own, att_sib, dq_sib = outs[:4]
    dkv = outs[4 : 4 + chips]
    q_all, g_all, weights_t, grads_t = outs[4 + chips :]
    rows = q_own.shape[0]
    span = 2 * rows
    scale = HD**-0.5
    chip, core = place[0], place[1]

    def body(blocks):
        k_t = [kv[b][0, :, :HD].T for b in range(blocks)]
        v_t = [kv[b][0, :, HD:].T for b in range(blocks)]
        key_at = lax.broadcasted_iota(jnp.int32, (span, span), 0)
        query_at = lax.broadcasted_iota(jnp.int32, (span, span), 1)
        swap = rows * core

        def position(at):
            return jnp.where(at < rows, at + swap, at - swap)

        visible = position(query_at) >= position(key_at)

        def head(j, _):
            lanes = pl.ds(pl.multiple_of(j * HD, HD), HD)
            base = pl.multiple_of(j * span, span)
            columns = pl.ds(base, span)
            query = jnp.concatenate([q_own[:, lanes], q_sib[:, lanes]], 0)
            grad = jnp.concatenate([g_own[:, lanes], g_sib[:, lanes]], 0)
            q_all[columns, :] = query
            g_all[columns, :] = grad
            scores = [dot(kv[b][0, :, :HD], query, NT) for b in range(blocks)]
            scores[0] = jnp.where(visible, scores[0], -jnp.inf)
            peak = functools.reduce(
                jnp.maximum, [jnp.max(s, axis=0, keepdims=True) for s in scores]
            )
            expo = [jnp.exp2((s - peak) * (scale * LOG2E)) for s in scores]
            total = sum(jnp.sum(e, axis=0, keepdims=True) for e in expo)
            inverse = 1.0 / total
            weights = [e * inverse for e in expo]
            low = [w.astype(jnp.bfloat16) for w in weights]
            for b in range(blocks):
                weights_t[b * span : (b + 1) * span, columns] = low[b]
            attended_t = sum(dot(v_t[b], low[b]) for b in range(blocks))
            attended_t = attended_t.astype(jnp.bfloat16)
            grad_t = grad.T
            row_dots = jnp.sum(
                grad_t.astype(jnp.float32) * attended_t.astype(jnp.float32),
                axis=0,
                keepdims=True,
            )
            query_grad_t = jnp.zeros((HD, span), jnp.float32)
            for b in range(blocks):
                weight_grads = dot(kv[b][0, :, HD:], grad_t)
                score_grads = (weights[b] * (weight_grads - row_dots)).astype(jnp.bfloat16)
                grads_t[b * span : (b + 1) * span, columns] = score_grads
                query_grad_t += dot(k_t[b], score_grads)
            attended = attended_t.T
            query_grad = (query_grad_t * scale).astype(jnp.bfloat16).T
            att_own[:, lanes] = attended[:rows]
            att_sib[:, lanes] = attended[rows:]
            dq_own[:, lanes] = query_grad[:rows]
            dq_sib[:, lanes] = query_grad[rows:]
            return _

        lax.fori_loop(0, heads, head, 0)

        for b in range(blocks):
            block = slice(b * span, (b + 1) * span)
            key_grad = dot(grads_t[block, :], q_all[...]) * scale
            value_grad = dot(weights_t[block, :], g_all[...])
            dkv[b][0, :, :HD] = key_grad.astype(dkv[b].dtype)
            dkv[b][0, :, HD:] = value_grad.astype(dkv[b].dtype)

    for c in range(chips):
        pl.when(chip == c)(functools.partial(body, c + 1))


def attention(place, first, count, queries, grads, kv, carried):
    query, query_sib = queries
    grad, grad_sib = grads
    rows, width = query.shape
    group = width // KVH
    heads = group // HD
    per_core = KVH // CORES
    chips = len(kv)
    span = 2 * rows

    def full(h, s):
        return (0, s[1] * per_core + first + h)

    def half(h, s):
        return (0, first + h)

    def whole(h, s):
        return (h, 0, 0)

    wide = pl.BlockSpec((rows, group), full)
    narrow = pl.BlockSpec((rows, group), half)
    kv_spec = pl.BlockSpec((1, span, 2 * HD), whole)
    in_specs = [wide, narrow, wide, narrow] + [kv_spec] * chips
    in_specs += [pl.BlockSpec(memory_space=pl.ANY)] * len(carried)
    half_width = per_core * group
    bf = jnp.bfloat16
    out_shape = [
        jax.ShapeDtypeStruct((rows, width), bf),
        jax.ShapeDtypeStruct((rows, width), bf),
        jax.ShapeDtypeStruct((rows, half_width), bf),
        jax.ShapeDtypeStruct((rows, half_width), bf),
    ] + [
        jax.ShapeDtypeStruct((count, span, 2 * HD), jnp.float32 if b == 0 else bf)
        for b in range(chips)
    ]
    out_specs = [wide, wide, narrow, narrow] + [kv_spec] * chips
    first_carried = 1 + 4 + chips
    results = pl.pallas_call(
        functools.partial(attention_kernel, chips, heads, len(carried)),
        grid_spec=pltpu.PrefetchScalarGridSpec(
            num_scalar_prefetch=1,
            grid=(count,),
            in_specs=in_specs,
            out_specs=out_specs,
            scratch_shapes=[
                pltpu.VMEM((heads * span, HD), bf),
                pltpu.VMEM((heads * span, HD), bf),
                pltpu.VMEM((chips * span, heads * span), bf),
                pltpu.VMEM((chips * span, heads * span), bf),
            ],
        ),
        out_shape=out_shape,
        input_output_aliases={first_carried + i: i for i in range(len(carried))},
        compiler_params=pltpu.CompilerParams(vmem_limit_bytes=52 * 2**20),
        cost_estimate=pl.CostEstimate(
            flops=count * 12 * heads * span * span * chips * HD,
            bytes_accessed=count * (8 * rows * group * 2 + 2 * chips * span * 2 * HD * 2),
            transcendentals=count * heads * span * span * chips,
        ),
        name=f"attention_{first}",
    )(place, query, query_sib, grad, grad_sib, *kv, *carried)
    return results[:4], results[4:]


def shards(query, keys, values, out_grad):
    devices = lax.axis_size("seq")
    chips = devices // CORES
    rows = query.shape[0]
    me = lax.axis_index("seq")
    chip, core = me // CORES, me % CORES
    place = jnp.stack([chip, core]).astype(jnp.int32)
    per_core = KVH // CORES
    sibling = [(i, i ^ 1) for i in range(devices)]

    def onward(d):
        return [(i, i + CORES * d) for i in range(devices - CORES * d)]

    def back(d):
        return [(i + CORES * d, i) for i in range(devices - CORES * d)]

    packed = jnp.stack(
        [
            jnp.concatenate(
                [keys[:, h * HD : (h + 1) * HD], values[:, h * HD : (h + 1) * HD]], 1
            )
            for h in range(KVH)
        ]
    )
    mine = lax.dynamic_slice_in_dim(packed, core * per_core, per_core, 0)
    theirs = lax.dynamic_slice_in_dim(packed, (1 - core) * per_core, per_core, 0)
    kv_own = jnp.concatenate([mine, lax.ppermute(theirs, "seq", sibling)], 1)

    kv = []
    first = 0
    for count in GROUPS:
        part = kv_own[first : first + count]
        kv.append([part] + [lax.ppermute(part, "seq", onward(d)) for d in range(1, chips)])
        first += count

    half = query.shape[1] // CORES

    def other(tensor):
        piece = lax.dynamic_slice_in_dim(tensor, (1 - core) * half, half, 1)
        return lax.ppermute(piece, "seq", sibling)

    query_sib, grad_sib = other(query), other(out_grad)

    carried = ()
    first = 0
    sums = []
    for count, blocks in zip(GROUPS, kv):
        carried, dkv = attention(
            place, first, count, (query, query_sib), (out_grad, grad_sib), blocks, carried
        )
        sums.append(
            [dkv[0]] + [lax.ppermute(dkv[d], "seq", back(d)) for d in range(1, chips)]
        )
        first += count

    attended, query_grad, att_sib, dq_sib = carried

    def placed_back(tensor, piece):
        arrived = lax.ppermute(piece, "seq", sibling)
        return lax.dynamic_update_slice_in_dim(tensor, arrived, (1 - core) * half, 1)

    attended = placed_back(attended, att_sib)
    query_grad = placed_back(query_grad, dq_sib)

    total = jnp.concatenate(
        [sum(part.astype(jnp.float32) for part in group) for group in sums], 0
    ).astype(jnp.bfloat16)
    ours, others = total[:, :rows], total[:, rows:]
    arrived = lax.ppermute(others, "seq", sibling)
    low = jnp.where(core == 0, ours, arrived)
    high = jnp.where(core == 0, arrived, ours)
    both = jnp.concatenate([low, high], 0)
    key_grad = both[:, :, :HD].transpose(1, 0, 2).reshape(rows, KVH * HD)
    value_grad = both[:, :, HD:].transpose(1, 0, 2).reshape(rows, KVH * HD)
    return attended, query_grad, key_grad, value_grad


def solution(mesh):
    spec = P(("dp", "seq"), None)
    return jax.shard_map(
        shards, mesh=mesh, in_specs=(spec,) * 4, out_specs=(spec,) * 4, check_vma=False
    )
```

```python
import functools

import jax
import jax.numpy as jnp
from jax import lax
from jax.experimental import pallas as pl
from jax.experimental.pallas import tpu as pltpu
from jax.sharding import PartitionSpec as P

KVH = 8
HD = 128
CORES = 2
TOGETHER = 2
LOG2E = 1.4426950408889634
SENT = (2, 2)
CALLS = (2, 2)
BACK = (2, 2)


def dot(a, b, dims=(((1,), (0,)), ((), ()))):
    return lax.dot_general(a, b, dims, preferred_element_type=jnp.float32)


NT = (((1,), (1,)), ((), ()))


def attention_kernel(chips, heads, n_alias, place, *refs):
    q_own, q_sib, g_own, g_sib = refs[:4]
    kv = refs[4 : 4 + chips]
    outs = refs[4 + chips + n_alias :]
    att_own, dq_own, att_sib, dq_sib = outs[:4]
    dkv = outs[4 : 4 + chips]
    q_all, g_all, weights_t, grads_t, inverses = outs[4 + chips :]
    rows = q_own.shape[0]
    span = 2 * rows
    scale = HD**-0.5
    chip, core = place[0], place[1]
    wide = TOGETHER * span

    def body(blocks):
        k_t = [kv[b][0, :, :HD].T for b in range(blocks)]
        v_t = [kv[b][0, :, HD:].T for b in range(blocks)]
        key_at = lax.broadcasted_iota(jnp.int32, (span, wide), 0)
        query_at = lax.broadcasted_iota(jnp.int32, (span, wide), 1) & (span - 1)
        swap = rows * core

        def position(at):
            return jnp.where(at < rows, at + swap, at - swap)

        visible = position(query_at) >= position(key_at)
        for j in range(heads):
            lanes = slice(j * HD, (j + 1) * HD)
            q_all[j * span : j * span + rows, :] = q_own[:, lanes]
            q_all[j * span + rows : (j + 1) * span, :] = q_sib[:, lanes]
            g_all[j * span : j * span + rows, :] = g_own[:, lanes]
            g_all[j * span + rows : (j + 1) * span, :] = g_sib[:, lanes]

        def forward(i):
            columns = pl.ds(pl.multiple_of(i * wide, wide), wide)
            query = q_all[columns, :]
            scores = [dot(kv[b][0, :, :HD], query, NT) for b in range(blocks)]
            yield
            scores[0] = jnp.where(visible, scores[0], -jnp.inf)
            peak = functools.reduce(
                jnp.maximum, [jnp.max(s, axis=0, keepdims=True) for s in scores]
            )
            total = jnp.zeros((1, wide), jnp.float32)
            for b in range(blocks):
                expo = jnp.exp2((scores[b] - peak) * (scale * LOG2E))
                total += jnp.sum(expo, axis=0, keepdims=True)
                weights_t[b * span : (b + 1) * span, columns] = expo.astype(jnp.bfloat16)
            inverses[:, columns] = 1.0 / total
            yield

        def backward(i):
            columns = pl.ds(pl.multiple_of(i * wide, wide), wide)
            inverse = inverses[:, columns]
            grad_t = g_all[columns, :].T
            grad_t = (grad_t.astype(jnp.float32) * inverse).astype(jnp.bfloat16)
            g_all[columns, :] = grad_t.T
            attended_t = jnp.zeros((HD, wide), jnp.float32)
            for b in range(blocks):
                attended_t += dot(v_t[b], weights_t[b * span : (b + 1) * span, columns])
            weight_grads = [dot(kv[b][0, :, HD:], grad_t) for b in range(blocks)]
            yield
            attended_t = (attended_t * inverse).astype(jnp.bfloat16)
            row_dots = jnp.sum(
                grad_t.astype(jnp.float32) * attended_t.astype(jnp.float32),
                axis=0,
                keepdims=True,
            )
            for b in range(blocks):
                block = slice(b * span, (b + 1) * span)
                score_grads = weights_t[block, columns].astype(jnp.float32) * (
                    weight_grads[b] - row_dots
                )
                grads_t[block, columns] = score_grads.astype(jnp.bfloat16)
            yield
            query_grad_t = jnp.zeros((HD, wide), jnp.float32)
            for b in range(blocks):
                block = slice(b * span, (b + 1) * span)
                query_grad_t += dot(k_t[b], grads_t[block, columns])
            attended = attended_t.T
            query_grad = (query_grad_t * scale).astype(jnp.bfloat16).T
            for t in range(TOGETHER):
                lanes = pl.ds(pl.multiple_of((i * TOGETHER + t) * HD, HD), HD)
                own = slice(t * span, t * span + rows)
                sib = slice(t * span + rows, (t + 1) * span)
                att_own[:, lanes] = attended[own]
                att_sib[:, lanes] = attended[sib]
                dq_own[:, lanes] = query_grad[own]
                dq_sib[:, lanes] = query_grad[sib]
            yield

        def run(running, stages):
            for _ in range(stages):
                next(running)

        def paired(i, _):
            f0, f1, b0, b1 = forward(2 * i), forward(2 * i + 1), backward(2 * i), backward(2 * i + 1)
            run(f0, 1)
            run(f1, 1)
            run(f0, 1)
            run(b0, 1)
            run(f1, 1)
            run(b1, 1)
            run(b0, 1)
            run(b0, 1)
            run(b1, 2)
            return _

        lax.fori_loop(0, heads // TOGETHER // 2, paired, 0)

        for b in range(blocks):
            block = slice(b * span, (b + 1) * span)
            key_grad = dot(grads_t[block, :], q_all[...]) * scale
            value_grad = dot(weights_t[block, :], g_all[...])
            dkv[b][0, :, :HD] = key_grad.astype(dkv[b].dtype)
            dkv[b][0, :, HD:] = value_grad.astype(dkv[b].dtype)

    for c in range(chips):
        pl.when(chip == c)(functools.partial(body, c + 1))


def attention(place, first, inside, count, queries, grads, kv, carried):
    query, query_sib = queries
    grad, grad_sib = grads
    rows, width = query.shape
    group = width // KVH
    heads = group // HD
    per_core = KVH // CORES
    chips = len(kv)
    span = 2 * rows

    def full(h, s):
        return (0, s[1] * per_core + first + h)

    def half(h, s):
        return (0, first + h)

    def whole(h, s):
        return (h, 0, 0)

    def arrived(h, s):
        return (inside + h, 0, 0)

    wide = pl.BlockSpec((rows, group), full)
    narrow = pl.BlockSpec((rows, group), half)
    kv_spec = pl.BlockSpec((1, span, 2 * HD), whole)
    in_specs = [wide, narrow, wide, narrow] + [pl.BlockSpec((1, span, 2 * HD), arrived)] * chips
    in_specs += [pl.BlockSpec(memory_space=pl.ANY)] * len(carried)
    half_width = width // CORES
    bf = jnp.bfloat16
    out_shape = [
        jax.ShapeDtypeStruct((rows, width), bf),
        jax.ShapeDtypeStruct((rows, width), bf),
        jax.ShapeDtypeStruct((rows, half_width), bf),
        jax.ShapeDtypeStruct((rows, half_width), bf),
    ] + [
        jax.ShapeDtypeStruct((count, span, 2 * HD), jnp.float32 if b == 0 else bf)
        for b in range(chips)
    ]
    out_specs = [wide, wide, narrow, narrow] + [kv_spec] * chips
    first_carried = 1 + 4 + chips
    results = pl.pallas_call(
        functools.partial(attention_kernel, chips, heads, len(carried)),
        grid_spec=pltpu.PrefetchScalarGridSpec(
            num_scalar_prefetch=1,
            grid=(count,),
            in_specs=in_specs,
            out_specs=out_specs,
            scratch_shapes=[
                pltpu.VMEM((heads * span, HD), bf),
                pltpu.VMEM((heads * span, HD), bf),
                pltpu.VMEM((chips * span, heads * span), bf),
                pltpu.VMEM((chips * span, heads * span), bf),
                pltpu.VMEM((1, heads * span), jnp.float32),
            ],
        ),
        out_shape=out_shape,
        input_output_aliases={first_carried + i: i for i in range(len(carried))},
        compiler_params=pltpu.CompilerParams(vmem_limit_bytes=52 * 2**20),
        cost_estimate=pl.CostEstimate(
            flops=count * 12 * heads * span * span * chips * HD,
            bytes_accessed=count * (8 * rows * group * 2 + 2 * chips * span * 2 * HD * 2),
            transcendentals=count * heads * span * span * chips,
        ),
        name=f"attention_{first}",
    )(place, query, query_sib, grad, grad_sib, *kv, *carried)
    return results[:4], results[4:]


def shards(query, keys, values, out_grad):
    devices = lax.axis_size("seq")
    chips = devices // CORES
    rows = query.shape[0]
    me = lax.axis_index("seq")
    chip, core = me // CORES, me % CORES
    place = jnp.stack([chip, core]).astype(jnp.int32)
    per_core = KVH // CORES
    sibling = [(i, i ^ 1) for i in range(devices)]

    def onward(d):
        return [(i, i + CORES * d) for i in range(devices - CORES * d)]

    def back(d):
        return [(i + CORES * d, i) for i in range(devices - CORES * d)]

    packed = jnp.stack(
        [
            jnp.concatenate(
                [keys[:, h * HD : (h + 1) * HD], values[:, h * HD : (h + 1) * HD]], 1
            )
            for h in range(KVH)
        ]
    )
    mine = lax.dynamic_slice_in_dim(packed, core * per_core, per_core, 0)
    theirs = lax.dynamic_slice_in_dim(packed, (1 - core) * per_core, per_core, 0)
    kv_own = jnp.concatenate([mine, lax.ppermute(theirs, "seq", sibling)], 1)

    kv = {}
    first = 0
    for count in SENT:
        part = kv_own[first : first + count]
        blocks = [part] + [lax.ppermute(part, "seq", onward(d)) for d in range(chips - 1, 0, -1)][::-1]
        for h in range(count):
            kv[first + h] = (h, blocks)
        first += count

    half = query.shape[1] // CORES
    kv_own, late_query, late_grad = lax.optimization_barrier((kv_own, query, out_grad))

    def other(tensor):
        piece = lax.dynamic_slice_in_dim(tensor, (1 - core) * half, half, 1)
        return lax.ppermute(piece, "seq", sibling)

    query_sib, grad_sib = other(late_query), other(late_grad)

    carried = ()
    parts = []
    first = 0
    for count in CALLS:
        inside, blocks = kv[first]
        carried, dkv = attention(
            place, first, inside, count, (query, query_sib), (out_grad, grad_sib), blocks, carried
        )
        parts += [[d[h : h + 1] for d in dkv] for h in range(count)]
        first += count

    attended, query_grad, att_sib, dq_sib = carried

    totals = []
    first = 0
    for count in BACK:
        group = [
            jnp.concatenate([parts[h][d] for h in range(first, first + count)], 0)
            for d in range(chips)
        ]
        total = group[0]
        for d in range(chips - 1, 0, -1):
            total = total + lax.ppermute(group[d], "seq", back(d)).astype(jnp.float32)
        total = total.astype(jnp.bfloat16)
        arrived = lax.ppermute(total[:, rows:], "seq", sibling)
        totals.append((total[:, :rows], arrived))
        first += count

    def placed_back(tensor, piece):
        arrived = lax.ppermute(piece, "seq", sibling)
        return lax.dynamic_update_slice_in_dim(tensor, arrived, (1 - core) * half, 1)

    attended = placed_back(attended, att_sib)
    query_grad = placed_back(query_grad, dq_sib)

    ours = [o[h] for o, _ in totals for h in range(o.shape[0])]
    arrived = [a[h] for _, a in totals for h in range(a.shape[0])]
    low = [jnp.where(core == 0, o, a) for o, a in zip(ours, arrived)]
    high = [jnp.where(core == 0, a, o) for o, a in zip(ours, arrived)]
    both = low + high
    key_grad = jnp.concatenate([b[:, :HD] for b in both], 1)
    value_grad = jnp.concatenate([b[:, HD:] for b in both], 1)
    return attended, query_grad, key_grad, value_grad


def solution(mesh):
    spec = P(("dp", "seq"), None)
    return jax.shard_map(
        shards, mesh=mesh, in_specs=(spec,) * 4, out_specs=(spec,) * 4, check_vma=False
    )
```

```python
import functools

import jax
import jax.numpy as jnp
from jax import lax
from jax.experimental import pallas as pl
from jax.experimental.pallas import tpu as pltpu
from jax.sharding import PartitionSpec as P

KVH = 8
HD = 128
CORES = 2
TOGETHER = 2
LOG2E = 1.4426950408889634
SENT = (2, 2)
CALLS = (2, 2)
BACK = (2, 2)


def dot(a, b, dims=(((1,), (0,)), ((), ()))):
    return lax.dot_general(a, b, dims, preferred_element_type=jnp.float32)


NT = (((1,), (1,)), ((), ()))


def attention_kernel(chips, heads, n_alias, place, *refs):
    q_own, q_sib, g_own, g_sib = refs[:4]
    kv = refs[4 : 4 + chips]
    outs = refs[4 + chips + n_alias :]
    att_own, dq_own, att_sib, dq_sib = outs[:4]
    dkv = outs[4 : 4 + chips]
    q_all, g_all, weights_t, grads_t, inverses = outs[4 + chips :]
    rows = q_own.shape[0]
    span = 2 * rows
    scale = HD**-0.5
    chip, core = place[0], place[1]
    wide = TOGETHER * span

    def body(blocks):
        k_t = [kv[b][0, :, :HD].T for b in range(blocks)]
        v_t = [kv[b][0, :, HD:].T for b in range(blocks)]
        key_at = lax.broadcasted_iota(jnp.int32, (span, wide), 0)
        query_at = lax.broadcasted_iota(jnp.int32, (span, wide), 1) & (span - 1)
        swap = rows * core

        def position(at):
            return jnp.where(at < rows, at + swap, at - swap)

        visible = position(query_at) >= position(key_at)
        for j in range(heads):
            lanes = slice(j * HD, (j + 1) * HD)
            q_all[j * span : j * span + rows, :] = q_own[:, lanes]
            q_all[j * span + rows : (j + 1) * span, :] = q_sib[:, lanes]
            g_all[j * span : j * span + rows, :] = g_own[:, lanes]
            g_all[j * span + rows : (j + 1) * span, :] = g_sib[:, lanes]

        def forward(i):
            columns = pl.ds(pl.multiple_of(i * wide, wide), wide)
            query = q_all[columns, :]
            scores = [dot(kv[b][0, :, :HD], query, NT) for b in range(blocks)]
            yield
            scores[0] = jnp.where(visible, scores[0], -jnp.inf)
            peak = functools.reduce(
                jnp.maximum, [jnp.max(s, axis=0, keepdims=True) for s in scores]
            )
            total = jnp.zeros((1, wide), jnp.float32)
            for b in range(blocks):
                expo = jnp.exp2((scores[b] - peak) * (scale * LOG2E))
                total += jnp.sum(expo, axis=0, keepdims=True)
                weights_t[b * span : (b + 1) * span, columns] = expo.astype(jnp.bfloat16)
            inverses[:, columns] = 1.0 / total
            yield

        def backward(i):
            columns = pl.ds(pl.multiple_of(i * wide, wide), wide)
            inverse = inverses[:, columns]
            grad_t = g_all[columns, :].T
            grad_t = (grad_t.astype(jnp.float32) * inverse).astype(jnp.bfloat16)
            g_all[columns, :] = grad_t.T
            attended_t = jnp.zeros((HD, wide), jnp.float32)
            for b in range(blocks):
                attended_t += dot(v_t[b], weights_t[b * span : (b + 1) * span, columns])
            weight_grads = [dot(kv[b][0, :, HD:], grad_t) for b in range(blocks)]
            yield
            attended_t = (attended_t * inverse).astype(jnp.bfloat16)
            row_dots = jnp.sum(
                grad_t.astype(jnp.float32) * attended_t.astype(jnp.float32),
                axis=0,
                keepdims=True,
            )
            for b in range(blocks):
                block = slice(b * span, (b + 1) * span)
                score_grads = weights_t[block, columns].astype(jnp.float32) * (
                    weight_grads[b] - row_dots
                )
                grads_t[block, columns] = score_grads.astype(jnp.bfloat16)
            yield
            query_grad_t = jnp.zeros((HD, wide), jnp.float32)
            for b in range(blocks):
                block = slice(b * span, (b + 1) * span)
                query_grad_t += dot(k_t[b], grads_t[block, columns])
            attended = attended_t.T
            query_grad = (query_grad_t * scale).astype(jnp.bfloat16).T
            for t in range(TOGETHER):
                lanes = pl.ds(pl.multiple_of((i * TOGETHER + t) * HD, HD), HD)
                own = slice(t * span, t * span + rows)
                sib = slice(t * span + rows, (t + 1) * span)
                att_own[:, lanes] = attended[own]
                att_sib[:, lanes] = attended[sib]
                dq_own[:, lanes] = query_grad[own]
                dq_sib[:, lanes] = query_grad[sib]
            yield

        def run(running, stages):
            for _ in range(stages):
                next(running)

        def paired(i, _):
            f0, f1, b0, b1 = forward(2 * i), forward(2 * i + 1), backward(2 * i), backward(2 * i + 1)
            run(f0, 1)
            run(f1, 1)
            run(f0, 1)
            run(b0, 1)
            run(f1, 1)
            run(b1, 1)
            run(b0, 1)
            run(b0, 1)
            run(b1, 2)
            return _

        lax.fori_loop(0, heads // TOGETHER // 2, paired, 0)

        for b in range(blocks):
            block = slice(b * span, (b + 1) * span)
            key_grad = dot(grads_t[block, :], q_all[...]) * scale
            value_grad = dot(weights_t[block, :], g_all[...])
            dkv[b][0, :, :HD] = key_grad.astype(dkv[b].dtype)
            dkv[b][0, :, HD:] = value_grad.astype(dkv[b].dtype)

    for c in range(chips):
        pl.when(chip == c)(functools.partial(body, c + 1))


def attention(place, first, inside, count, queries, grads, kv, carried):
    query, query_sib = queries
    grad, grad_sib = grads
    rows, width = query.shape
    group = width // KVH
    heads = group // HD
    per_core = KVH // CORES
    chips = len(kv)
    span = 2 * rows

    def full(h, s):
        return (0, s[1] * per_core + first + h)

    def half(h, s):
        return (0, first + h)

    def whole(h, s):
        return (h, 0, 0)

    def arrived(h, s):
        return (inside + h, 0, 0)

    wide = pl.BlockSpec((rows, group), full)
    narrow = pl.BlockSpec((rows, group), half)
    kv_spec = pl.BlockSpec((1, span, 2 * HD), whole)
    in_specs = [wide, narrow, wide, narrow] + [pl.BlockSpec((1, span, 2 * HD), arrived)] * chips
    in_specs += [pl.BlockSpec(memory_space=pl.ANY)] * len(carried)
    half_width = width // CORES
    bf = jnp.bfloat16
    out_shape = [
        jax.ShapeDtypeStruct((rows, width), bf),
        jax.ShapeDtypeStruct((rows, width), bf),
        jax.ShapeDtypeStruct((rows, half_width), bf),
        jax.ShapeDtypeStruct((rows, half_width), bf),
    ] + [
        jax.ShapeDtypeStruct((count, span, 2 * HD), jnp.float32 if b == 0 else bf)
        for b in range(chips)
    ]
    out_specs = [wide, wide, narrow, narrow] + [kv_spec] * chips
    first_carried = 1 + 4 + chips
    results = pl.pallas_call(
        functools.partial(attention_kernel, chips, heads, len(carried)),
        grid_spec=pltpu.PrefetchScalarGridSpec(
            num_scalar_prefetch=1,
            grid=(count,),
            in_specs=in_specs,
            out_specs=out_specs,
            scratch_shapes=[
                pltpu.VMEM((heads * span, HD), bf),
                pltpu.VMEM((heads * span, HD), bf),
                pltpu.VMEM((chips * span, heads * span), bf),
                pltpu.VMEM((chips * span, heads * span), bf),
                pltpu.VMEM((1, heads * span), jnp.float32),
            ],
        ),
        out_shape=out_shape,
        input_output_aliases={first_carried + i: i for i in range(len(carried))},
        compiler_params=pltpu.CompilerParams(vmem_limit_bytes=52 * 2**20),
        cost_estimate=pl.CostEstimate(
            flops=count * 12 * heads * span * span * chips * HD,
            bytes_accessed=count * (8 * rows * group * 2 + 2 * chips * span * 2 * HD * 2),
            transcendentals=count * heads * span * span * chips,
        ),
        name=f"attention_{first}",
    )(place, query, query_sib, grad, grad_sib, *kv, *carried)
    return results[:4], results[4:]


def shards(query, keys, values, out_grad):
    devices = lax.axis_size("seq")
    chips = devices // CORES
    rows = query.shape[0]
    me = lax.axis_index("seq")
    chip, core = me // CORES, me % CORES
    place = jnp.stack([chip, core]).astype(jnp.int32)
    per_core = KVH // CORES
    sibling = [(i, i ^ 1) for i in range(devices)]

    def onward(d):
        return [(i, i + CORES * d) for i in range(devices - CORES * d)]

    def back(d):
        return [(i + CORES * d, i) for i in range(devices - CORES * d)]

    packed = jnp.stack(
        [
            jnp.concatenate(
                [keys[:, h * HD : (h + 1) * HD], values[:, h * HD : (h + 1) * HD]], 1
            )
            for h in range(KVH)
        ]
    )
    mine = lax.dynamic_slice_in_dim(packed, core * per_core, per_core, 0)
    theirs = lax.dynamic_slice_in_dim(packed, (1 - core) * per_core, per_core, 0)
    kv_own = jnp.concatenate([mine, lax.ppermute(theirs, "seq", sibling)], 1)

    half = query.shape[1] // CORES

    def other(tensor):
        piece = lax.dynamic_slice_in_dim(tensor, (1 - core) * half, half, 1)
        return lax.ppermute(piece, "seq", sibling)

    query_sib, grad_sib = other(query), other(out_grad)

    kv = {}
    first = 0
    for count in SENT:
        part = kv_own[first : first + count]
        if first:
            part, *arrived = lax.optimization_barrier((part, *blocks[1:]))
            blocks[1:] = arrived
        blocks = [part] + [lax.ppermute(part, "seq", onward(d)) for d in range(1, chips)]
        for h in range(count):
            kv[first + h] = (h, blocks)
        first += count

    carried = ()
    parts = []
    first = 0
    for count in CALLS:
        inside, blocks = kv[first]
        carried, dkv = attention(
            place, first, inside, count, (query, query_sib), (out_grad, grad_sib), blocks, carried
        )
        parts += [[d[h : h + 1] for d in dkv] for h in range(count)]
        first += count

    attended, query_grad, att_sib, dq_sib = carried

    returned = []
    first = 0
    for count in BACK:
        group = [
            jnp.concatenate([parts[h][d] for h in range(first, first + count)], 0)
            for d in range(chips)
        ]
        returned.append(
            [group[0]] + [lax.ppermute(group[d], "seq", back(d)) for d in range(1, chips)]
        )
        first += count
    returned[:-1], att_sib = lax.optimization_barrier((returned[:-1], att_sib))

    totals = []
    for group in returned:
        total = group[0]
        for d in range(chips - 1, 0, -1):
            total = total + group[d].astype(jnp.float32)
        total = total.astype(jnp.bfloat16)
        arrived = lax.ppermute(total[:, rows:], "seq", sibling)
        totals.append((total[:, :rows], arrived))

    def placed_back(tensor, piece):
        arrived = lax.ppermute(piece, "seq", sibling)
        return lax.dynamic_update_slice_in_dim(tensor, arrived, (1 - core) * half, 1)

    attended = placed_back(attended, att_sib)
    query_grad = placed_back(query_grad, dq_sib)

    ours = [o[h] for o, _ in totals for h in range(o.shape[0])]
    arrived = [a[h] for _, a in totals for h in range(a.shape[0])]
    low = [jnp.where(core == 0, o, a) for o, a in zip(ours, arrived)]
    high = [jnp.where(core == 0, a, o) for o, a in zip(ours, arrived)]
    both = low + high
    key_grad = jnp.concatenate([b[:, :HD] for b in both], 1)
    value_grad = jnp.concatenate([b[:, HD:] for b in both], 1)
    return attended, query_grad, key_grad, value_grad


def solution(mesh):
    spec = P(("dp", "seq"), None)
    return jax.shard_map(
        shards, mesh=mesh, in_specs=(spec,) * 4, out_specs=(spec,) * 4, check_vma=False
    )
```

```python
import functools

import jax
import jax.numpy as jnp
from jax import lax
from jax.experimental import pallas as pl
from jax.experimental.pallas import tpu as pltpu
from jax.sharding import PartitionSpec as P

KVH = 8
HD = 128
CORES = 2
TOGETHER = 2
LOG2E = 1.4426950408889634
SENT = (2, 2)
CALLS = (2, 2)
BACK = (2, 2)


def dot(a, b, dims=(((1,), (0,)), ((), ()))):
    return lax.dot_general(a, b, dims, preferred_element_type=jnp.float32)


NT = (((1,), (1,)), ((), ()))


def attention_kernel(chips, heads, n_alias, place, *refs):
    q_own, q_sib, g_own, g_sib = refs[:4]
    kv = refs[4 : 4 + chips]
    outs = refs[4 + chips + n_alias :]
    att_own, dq_own, att_sib, dq_sib = outs[:4]
    dkv = outs[4 : 4 + chips]
    q_all, g_all, weights_t, grads_t, inverses = outs[4 + chips :]
    rows = q_own.shape[0]
    span = 2 * rows
    scale = HD**-0.5
    chip, core = place[0], place[1]
    wide = TOGETHER * span

    def body(blocks):
        k_t = [kv[b][0, :, :HD].T for b in range(blocks)]
        v_t = [kv[b][0, :, HD:].T for b in range(blocks)]
        key_at = lax.broadcasted_iota(jnp.int32, (span, wide), 0)
        query_at = lax.broadcasted_iota(jnp.int32, (span, wide), 1) & (span - 1)
        swap = rows * core

        def position(at):
            return jnp.where(at < rows, at + swap, at - swap)

        visible = position(query_at) >= position(key_at)
        for j in range(heads):
            lanes = slice(j * HD, (j + 1) * HD)
            q_all[j * span : j * span + rows, :] = q_own[:, lanes]
            q_all[j * span + rows : (j + 1) * span, :] = q_sib[:, lanes]
            g_all[j * span : j * span + rows, :] = g_own[:, lanes]
            g_all[j * span + rows : (j + 1) * span, :] = g_sib[:, lanes]

        def forward(i):
            columns = pl.ds(pl.multiple_of(i * wide, wide), wide)
            query = q_all[columns, :]
            scores = [dot(kv[b][0, :, :HD], query, NT) for b in range(blocks)]
            yield
            scores[0] = jnp.where(visible, scores[0], -jnp.inf)
            peak = functools.reduce(
                jnp.maximum, [jnp.max(s, axis=0, keepdims=True) for s in scores]
            )
            total = jnp.zeros((1, wide), jnp.float32)
            for b in range(blocks):
                expo = jnp.exp2((scores[b] - peak) * (scale * LOG2E))
                total += jnp.sum(expo, axis=0, keepdims=True)
                weights_t[b * span : (b + 1) * span, columns] = expo.astype(jnp.bfloat16)
            inverses[:, columns] = 1.0 / total
            yield

        def backward(i):
            columns = pl.ds(pl.multiple_of(i * wide, wide), wide)
            inverse = inverses[:, columns]
            grad_t = g_all[columns, :].T
            grad_t = (grad_t.astype(jnp.float32) * inverse).astype(jnp.bfloat16)
            g_all[columns, :] = grad_t.T
            attended_t = jnp.zeros((HD, wide), jnp.float32)
            for b in range(blocks):
                attended_t += dot(v_t[b], weights_t[b * span : (b + 1) * span, columns])
            weight_grads = [dot(kv[b][0, :, HD:], grad_t) for b in range(blocks)]
            yield
            attended_t = (attended_t * inverse).astype(jnp.bfloat16)
            row_dots = jnp.sum(
                grad_t.astype(jnp.float32) * attended_t.astype(jnp.float32),
                axis=0,
                keepdims=True,
            )
            for b in range(blocks):
                block = slice(b * span, (b + 1) * span)
                score_grads = weights_t[block, columns].astype(jnp.float32) * (
                    weight_grads[b] - row_dots
                )
                grads_t[block, columns] = score_grads.astype(jnp.bfloat16)
            yield
            query_grad_t = jnp.zeros((HD, wide), jnp.float32)
            for b in range(blocks):
                block = slice(b * span, (b + 1) * span)
                query_grad_t += dot(k_t[b], grads_t[block, columns])
            attended = attended_t.T
            query_grad = (query_grad_t * scale).astype(jnp.bfloat16).T
            for t in range(TOGETHER):
                lanes = pl.ds(pl.multiple_of((i * TOGETHER + t) * HD, HD), HD)
                own = slice(t * span, t * span + rows)
                sib = slice(t * span + rows, (t + 1) * span)
                att_own[:, lanes] = attended[own]
                att_sib[:, lanes] = attended[sib]
                dq_own[:, lanes] = query_grad[own]
                dq_sib[:, lanes] = query_grad[sib]
            yield

        def run(running, stages):
            for _ in range(stages):
                next(running)

        def paired(i, _):
            f0, f1, b0, b1 = forward(2 * i), forward(2 * i + 1), backward(2 * i), backward(2 * i + 1)
            run(f0, 1)
            run(f1, 1)
            run(f0, 1)
            run(b0, 1)
            run(f1, 1)
            run(b1, 1)
            run(b0, 1)
            run(b0, 1)
            run(b1, 2)
            return _

        lax.fori_loop(0, heads // TOGETHER // 2, paired, 0)

        for b in range(blocks):
            block = slice(b * span, (b + 1) * span)
            key_grad = dot(grads_t[block, :], q_all[...]) * scale
            value_grad = dot(weights_t[block, :], g_all[...])
            dkv[b][0, :, :HD] = key_grad.astype(dkv[b].dtype)
            dkv[b][0, :, HD:] = value_grad.astype(dkv[b].dtype)

    for c in range(chips):
        pl.when(chip == c)(functools.partial(body, c + 1))


def attention(place, first, inside, count, queries, grads, kv, carried):
    query, query_sib = queries
    grad, grad_sib = grads
    rows, width = query.shape
    group = width // KVH
    heads = group // HD
    per_core = KVH // CORES
    chips = len(kv)
    span = 2 * rows

    def full(h, s):
        return (0, s[1] * per_core + first + h)

    def half(h, s):
        return (0, first + h)

    def whole(h, s):
        return (h, 0, 0)

    def arrived(h, s):
        return (inside + h, 0, 0)

    wide = pl.BlockSpec((rows, group), full)
    narrow = pl.BlockSpec((rows, group), half)
    kv_spec = pl.BlockSpec((1, span, 2 * HD), whole)
    in_specs = [wide, narrow, wide, narrow] + [pl.BlockSpec((1, span, 2 * HD), arrived)] * chips
    in_specs += [pl.BlockSpec(memory_space=pl.ANY)] * len(carried)
    half_width = width // CORES
    bf = jnp.bfloat16
    out_shape = [
        jax.ShapeDtypeStruct((rows, width), bf),
        jax.ShapeDtypeStruct((rows, width), bf),
        jax.ShapeDtypeStruct((rows, half_width), bf),
        jax.ShapeDtypeStruct((rows, half_width), bf),
    ] + [
        jax.ShapeDtypeStruct((count, span, 2 * HD), jnp.float32 if b == 0 else bf)
        for b in range(chips)
    ]
    out_specs = [wide, wide, narrow, narrow] + [kv_spec] * chips
    first_carried = 1 + 4 + chips
    results = pl.pallas_call(
        functools.partial(attention_kernel, chips, heads, len(carried)),
        grid_spec=pltpu.PrefetchScalarGridSpec(
            num_scalar_prefetch=1,
            grid=(count,),
            in_specs=in_specs,
            out_specs=out_specs,
            scratch_shapes=[
                pltpu.VMEM((heads * span, HD), bf),
                pltpu.VMEM((heads * span, HD), bf),
                pltpu.VMEM((chips * span, heads * span), bf),
                pltpu.VMEM((chips * span, heads * span), bf),
                pltpu.VMEM((1, heads * span), jnp.float32),
            ],
        ),
        out_shape=out_shape,
        input_output_aliases={first_carried + i: i for i in range(len(carried))},
        compiler_params=pltpu.CompilerParams(vmem_limit_bytes=52 * 2**20),
        cost_estimate=pl.CostEstimate(
            flops=count * 12 * heads * span * span * chips * HD,
            bytes_accessed=count * (8 * rows * group * 2 + 2 * chips * span * 2 * HD * 2),
            transcendentals=count * heads * span * span * chips,
        ),
        name=f"attention_{first}",
    )(place, query, query_sib, grad, grad_sib, *kv, *carried)
    return results[:4], results[4:]


def shards(query, keys, values, out_grad):
    devices = lax.axis_size("seq")
    chips = devices // CORES
    rows = query.shape[0]
    me = lax.axis_index("seq")
    chip, core = me // CORES, me % CORES
    place = jnp.stack([chip, core]).astype(jnp.int32)
    per_core = KVH // CORES
    sibling = [(i, i ^ 1) for i in range(devices)]

    def onward(d):
        return [(i, i + CORES * d) for i in range(devices - CORES * d)]

    def back(d):
        return [(i + CORES * d, i) for i in range(devices - CORES * d)]

    packed = jnp.stack(
        [
            jnp.concatenate(
                [keys[:, h * HD : (h + 1) * HD], values[:, h * HD : (h + 1) * HD]], 1
            )
            for h in range(KVH)
        ]
    )
    mine = lax.dynamic_slice_in_dim(packed, core * per_core, per_core, 0)
    theirs = lax.dynamic_slice_in_dim(packed, (1 - core) * per_core, per_core, 0)
    kv_own = jnp.concatenate([mine, lax.ppermute(theirs, "seq", sibling)], 1)

    half = query.shape[1] // CORES

    def other(tensor):
        return lax.dynamic_slice_in_dim(tensor, (1 - core) * half, half, 1)

    halves = other(query), other(out_grad)

    kv = {}
    first = 0
    for count in SENT:
        part = kv_own[first : first + count]
        if first:
            part, *arrived = lax.optimization_barrier((part, *blocks[1:]))
            blocks[1:] = arrived
        blocks = [part] + [lax.ppermute(part, "seq", onward(d)) for d in range(1, chips)]
        if not first:
            *halves, blocks[1:] = lax.optimization_barrier((*halves, blocks[1:]))
            query_sib, grad_sib = (lax.ppermute(h, "seq", sibling) for h in halves)
        for h in range(count):
            kv[first + h] = (h, blocks)
        first += count

    carried = ()
    parts = []
    first = 0
    for count in CALLS:
        inside, blocks = kv[first]
        carried, dkv = attention(
            place, first, inside, count, (query, query_sib), (out_grad, grad_sib), blocks, carried
        )
        parts += [[d[h : h + 1] for d in dkv] for h in range(count)]
        first += count

    attended, query_grad, att_sib, dq_sib = carried

    returned = []
    first = 0
    for count in BACK:
        group = [
            jnp.concatenate([parts[h][d] for h in range(first, first + count)], 0)
            for d in range(chips)
        ]
        returned.append(
            [group[0]] + [lax.ppermute(group[d], "seq", back(d)) for d in range(1, chips)]
        )
        first += count
    returned[:-1], att_sib = lax.optimization_barrier((returned[:-1], att_sib))

    totals = []
    for group in returned:
        total = group[0]
        for d in range(chips - 1, 0, -1):
            total = total + group[d].astype(jnp.float32)
        total = total.astype(jnp.bfloat16)
        arrived = lax.ppermute(total[:, rows:], "seq", sibling)
        totals.append((total[:, :rows], arrived))

    def placed_back(tensor, piece):
        arrived = lax.ppermute(piece, "seq", sibling)
        return lax.dynamic_update_slice_in_dim(tensor, arrived, (1 - core) * half, 1)

    attended = placed_back(attended, att_sib)
    query_grad = placed_back(query_grad, dq_sib)

    ours = [o[h] for o, _ in totals for h in range(o.shape[0])]
    arrived = [a[h] for _, a in totals for h in range(a.shape[0])]
    low = [jnp.where(core == 0, o, a) for o, a in zip(ours, arrived)]
    high = [jnp.where(core == 0, a, o) for o, a in zip(ours, arrived)]
    both = low + high
    key_grad = jnp.concatenate([b[:, :HD] for b in both], 1)
    value_grad = jnp.concatenate([b[:, HD:] for b in both], 1)
    return attended, query_grad, key_grad, value_grad


def solution(mesh):
    spec = P(("dp", "seq"), None)
    return jax.shard_map(
        shards, mesh=mesh, in_specs=(spec,) * 4, out_specs=(spec,) * 4, check_vma=False
    )
```
